32 devices in a mesh: side: 2 (over core), shard: 16 (over z, y, x).
Axes of the slice: x: 2, y: 2, z: 4, core: 2. Of those that a mesh axis runs over, the one named last changes fastest.
Arguments:
- sketch: bfloat16 [2, 32768, 128], P('side', 'shard'), may hold values from -6 to 6
- tile_values: bfloat16 [2, 81920, 1024], P('side', 'shard'), may hold values from -100 to 100, as said below
- sent_blocks: int32 [2, 640], P(None, 'shard'), may hold values from 0 to 15, as said below
- pair_counts: int32 [2, 80], P(None, 'shard'), may hold values from 4 to 8, as said below
Outputs:
- new_sketch: float32 [2, 32768, 128], P('side', 'shard')
The draws below stay inside these ranges and needn't reach their ends.
Inputs may be any that keep to these rules, and one draw needn't show every extreme that they name: The two sides hold one matrix: tile_values[1, o, j] is the transpose of tile_values[0, (o + j - 2) mod 16, 4 - j] in the layout of the first step. `sent_blocks`: the 8 entries of one side, owner and pair are distinct. `pair_counts`: for every side and owner some pair uses all 8 slots.
All inputs are finite; a program needn't handle non-finite values.
Results may differ from the reference program's by a relative error of at most 0.0003.
Values may be sent and summed in bfloat16 or wider, within the bound.
No kernel may reach another device: no remote copies, remote signals or barrier semaphores. Data moves between devices by JAX's collectives and lax.ppermute only.
A program may use at most 64 MiB of HBM per device.

```python
import math
import jax
import jax.numpy as jnp
from jax import lax

TB = 128
RANK = 128
BLK_DEV = 16
PEER = 8
HALF = 2
PAIRS = 5
OWNERS = 16
ROWS = 32768


def tile_pattern(key, flat_pair):
    extent = PEER * TB
    source = jax.random.fold_in(key, flat_pair)
    normal_key, row_key, column_key = jax.random.split(source, 3)
    values = jnp.clip(jax.random.normal(normal_key, (extent, extent), jnp.float32), -6.0, 6.0)
    spread = math.log(10.0)
    growth = 0.5 * math.log(3.0)
    row_scale = jnp.exp(jax.random.uniform(row_key, (extent,), jnp.float32, 0.0, spread))
    column_scale = jnp.exp(jax.random.uniform(column_key, (extent,), jnp.float32, 0.0, spread))
    owner_pos = (flat_pair // PAIRS).astype(jnp.float32)
    trend = jnp.exp(growth * owner_pos / max(OWNERS - 1, 1))
    scaled = values * row_scale[:, None] * column_scale[None, :] * trend / math.sqrt(PAIRS * PEER * TB)
    return jnp.clip(scaled, -100.0, 100.0)


def draw_tile_values(key, part):
    extent = PEER * TB
    count_pairs = OWNERS * PAIRS

    def user_side(flat_pair):
        return tile_pattern(key, flat_pair).astype(jnp.bfloat16)

    def item_side(flat_pair):
        owner_pos = flat_pair // PAIRS
        pair_pos = flat_pair % PAIRS
        partner = (owner_pos + pair_pos - HALF) % OWNERS
        return tile_pattern(key, partner * PAIRS + (PAIRS - 1 - pair_pos)).T.astype(jnp.bfloat16)
    flats = jnp.arange(count_pairs, dtype=jnp.int32)
    first = lax.map(user_side, flats)
    second = lax.map(item_side, flats)
    return jnp.stack([first, second]).reshape(2, count_pairs * extent, extent)


def draw_sent_blocks(key, part):
    own_key = jax.random.fold_in(key, 11)
    rows_total = 2 * OWNERS * PAIRS
    scores = jax.random.randint(own_key, (rows_total, BLK_DEV), 0, 2 ** 20, dtype=jnp.int32)
    scores = scores * BLK_DEV + jnp.arange(BLK_DEV, dtype=jnp.int32)[None, :]
    chosen = jnp.argsort(scores, axis=1)[:, :PEER]
    return chosen.astype(jnp.int32).reshape(2, OWNERS * PAIRS * PEER)


def draw_pair_counts(key, part):
    own_key = jax.random.fold_in(key, 23)
    count_key, full_key = jax.random.split(own_key, 2)
    counts = jax.random.randint(count_key, (2, OWNERS, PAIRS), PEER // 2, PEER + 1, dtype=jnp.int32)
    full_pair = jax.random.randint(full_key, (2, OWNERS, 1), 0, PAIRS, dtype=jnp.int32)
    places = jnp.arange(PAIRS, dtype=jnp.int32)[None, None, :]
    counts = jnp.where(places == full_pair, PEER, counts)
    return counts.astype(jnp.int32).reshape(2, OWNERS * PAIRS)


def levels(rng, dims, pieces, smallest, high):
    level = 1.0
    for position, parts in pieces:
        steps = jax.random.uniform(jax.random.fold_in(jax.random.fold_in(rng, 6), position), (parts,), jnp.float32, smallest / len(pieces), high / len(pieces))
        level = level * jnp.repeat(jnp.exp(steps), dims[position] // parts).reshape((-1,) + (1,) * (len(dims) - 1 - position))
    return level


def gaussian(key, shape, scale, reach, pieces=(), kind=jnp.bfloat16):
    result = scale * jax.random.normal(key, shape, jnp.float32)
    if pieces:
        result = result * levels(key, shape, pieces, -0.22, 0.18)
    return jnp.clip(result, -reach, reach).astype(kind)


def setup_inputs(seed: int = 0) -> dict:
    seeds = jax.random.split(jax.random.key(seed), 5)
    sketch = gaussian(seeds[0], (2, ROWS, RANK), 1.0, 6.0, ((0, 2), (1, 16)))
    tile_values = draw_tile_values(jax.random.fold_in(seeds[4], 71), 0)
    sent_blocks = draw_sent_blocks(jax.random.fold_in(seeds[4], 71), 0)
    pair_counts = draw_pair_counts(jax.random.fold_in(seeds[4], 71), 0)
    return dict(sketch=sketch, tile_values=tile_values, sent_blocks=sent_blocks, pair_counts=pair_counts)


EPSILON = 1e-05

def side_update(own_side, sketch, tile_values, sent_blocks, pair_counts):
    far_side = 1 - own_side
    block_lists = sent_blocks.reshape(2, OWNERS, PAIRS, PEER)
    block_counts = pair_counts.reshape(2, OWNERS, PAIRS)
    far_sketch = sketch[far_side].reshape(OWNERS, BLK_DEV, TB, RANK)
    tile_grid = tile_values[own_side].reshape(OWNERS, PAIRS, PEER * TB, PEER * TB)
    offsets = jnp.arange(PAIRS, dtype=jnp.int32) - HALF
    mirror = (PAIRS - 1 - jnp.arange(PAIRS, dtype=jnp.int32)).astype(jnp.int32)
    places = jnp.arange(PEER, dtype=jnp.int32)
    targets = jnp.arange(BLK_DEV, dtype=jnp.int32)

    def one_owner(owner_pos):
        partner = ((owner_pos + offsets) % OWNERS).astype(jnp.int32)
        far_lists = block_lists[far_side][partner, mirror]
        far_counts = block_counts[far_side][partner, mirror]
        fetched = far_sketch[partner[:, None], far_lists]
        usable_far = places[None, :] < far_counts[:, None]
        fetched = jnp.where(usable_far[:, :, None, None], fetched, jnp.zeros_like(fetched))
        fetched = fetched.reshape(PAIRS, PEER * TB, RANK).astype(jnp.float32)
        product = jnp.einsum('jab,jbr->jar', tile_grid[owner_pos].astype(jnp.float32), fetched, precision=lax.Precision.HIGHEST)
        own_lists = block_lists[own_side][owner_pos]
        own_counts = block_counts[own_side][owner_pos]
        usable_own = places[None, :] < own_counts[:, None]
        routing = ((own_lists[:, :, None] == targets[None, None, :]) & usable_own[:, :, None]).astype(jnp.float32)
        return jnp.einsum('jak,jatr->ktr', routing, product.reshape(PAIRS, PEER, TB, RANK), precision=lax.Precision.HIGHEST)
    update = lax.map(one_owner, jnp.arange(OWNERS, dtype=jnp.int32)).reshape(ROWS, RANK)
    gram_matrix = jnp.dot(update.T, update, precision=lax.Precision.HIGHEST) / ROWS
    gram_matrix = gram_matrix + EPSILON * jnp.eye(RANK, dtype=jnp.float32)
    factor = jnp.linalg.cholesky(gram_matrix)
    return jax.scipy.linalg.solve_triangular(factor, update.T, lower=True).T

def reference(sketch, tile_values, sent_blocks, pair_counts):
    users_new = side_update(0, sketch, tile_values, sent_blocks, pair_counts)
    items_new = side_update(1, sketch, tile_values, sent_blocks, pair_counts)
    return jnp.stack([users_new, items_new])
```

```python
import functools
import jax
import jax.numpy as jnp
from jax import lax
from jax.experimental import pallas as pl
from jax.experimental.pallas import tpu as pltpu
from jax.sharding import PartitionSpec as P

TB = 128
RANK = 128
PEER = 8
HALF = 2
PAIRS = 5
EXTENT = PEER * TB
EPSILON = 1e-05
SUB = 8
CHUNK = 256
MIB = 1 << 20

VMEM = pl.BlockSpec(memory_space=pltpu.VMEM)
SMEM = pl.BlockSpec(memory_space=pltpu.SMEM)
ANY = pl.BlockSpec(memory_space=pl.ANY)


def resident(x):
    return pltpu.with_memory_space_constraint(x, pltpu.VMEM)


def routes(owners):
    if owners % 4 == 0:
        up = [
            lambda o: (o // 2) % 2 == 0,
            lambda o: o % 2 == 1,
            lambda o: (o // 2) % 2 == 1,
            lambda o: o % 2 == 0,
        ]
        reach = [2, 1, 2, 1]
        made = []
        for is_up, by in zip(up, reach):
            partner = [(o + (by if is_up(o) else -by)) % owners for o in range(owners)]
            pair = [HALF + (by if is_up(o) else -by) for o in range(owners)]
            made.append((partner, pair, pair))
        return made
    made = []
    for by in (2, 1, -2, -1):
        partner = [(o + by) % owners for o in range(owners)]
        made.append((partner, [HALF + by] * owners, [HALF - by] * owners))
    return made


def pack_kernel(pair_ref, lists_ref, counts_ref, sketch_ref, *out_refs):
    for position, out_ref in enumerate(out_refs):
        pair = pair_ref[position]
        live = counts_ref[pair]
        for slot in range(PEER):
            block = lists_ref[pair * PEER + slot]
            rows = sketch_ref[pl.ds(pl.multiple_of(block * TB, TB), TB), :]
            out_ref[slot * TB : (slot + 1) * TB, :] = jnp.where(slot < live, rows, jnp.zeros_like(rows))


def add_product(pair, lists_ref, counts_ref, tile_chunk, fetched, update_ref, chunk):
    part = jnp.dot(tile_chunk, fetched, preferred_element_type=jnp.float32)
    for step in range(CHUNK // TB):
        slot = chunk * (CHUNK // TB) + step
        block = lists_ref[pair * PEER + slot]

        @pl.when(slot < counts_ref[pair])
        def _():
            rows = pl.ds(pl.multiple_of(block * TB, TB), TB)
            update_ref[rows, :] += part[step * TB : (step + 1) * TB, :]


def first_kernel(position, pair_ref, lists_ref, counts_ref, tile_ref, fetched_ref, update_ref, held, sems):
    update_ref[...] = jnp.zeros_like(update_ref)
    multiply(position, pair_ref, lists_ref, counts_ref, tile_ref, fetched_ref, update_ref, held, sems)


def next_kernel(position, pair_ref, lists_ref, counts_ref, tile_ref, fetched_ref, _, update_ref, held, sems):
    multiply(position, pair_ref, lists_ref, counts_ref, tile_ref, fetched_ref, update_ref, held, sems)


def multiply(position, pair_ref, lists_ref, counts_ref, tile_ref, fetched_ref, update_ref, held, sems):
    pair = pair_ref[position]
    copies = []
    for chunk in range(EXTENT // CHUNK):
        start = pl.multiple_of(pair * EXTENT + chunk * CHUNK, CHUNK)
        copy = pltpu.make_async_copy(tile_ref.at[pl.ds(start, CHUNK), :], held.at[chunk], sems.at[chunk])
        copy.start()
        copies.append(copy)
    fetched = fetched_ref[...]
    for chunk, copy in enumerate(copies):
        copy.wait()
        add_product(pair, lists_ref, counts_ref, held[chunk], fetched, update_ref, chunk)


def split(x):
    high = x.astype(jnp.bfloat16)
    low = (x - high.astype(jnp.float32)).astype(jnp.bfloat16)
    return high, low


def gram_kernel(update_ref, gram_ref):
    high, low = split(update_ref[...])
    down = (((0,), (0,)), ((), ()))
    dot = functools.partial(lax.dot_general, dimension_numbers=down, preferred_element_type=jnp.float32)
    gram_ref[...] = dot(high, high) + dot(high, low) + dot(low, high)


def refined(guess, value):
    for _ in range(2):
        guess = guess * (2.0 - value * guess)
    return guess


def factor_inverse(gram, put):
    width = gram.shape[1]
    blocks = width // SUB
    spread = lambda x: jnp.broadcast_to(x, (SUB, width))
    sub = lax.broadcasted_iota(jnp.int32, (SUB, width), 0)
    lane = lax.broadcasted_iota(jnp.int32, (SUB, width), 1)
    rows = [gram[i * SUB : (i + 1) * SUB, :] for i in range(blocks)]
    inverse = [jnp.where(lane == sub + i * SUB, 1.0, 0.0) for i in range(blocks)]
    for b in range(blocks):
        base = b * SUB
        columns = [spread(rows[b][:, base + r : base + r + 1]) for r in range(SUB)]
        m = [[spread(columns[j][i : i + 1, :]) if j <= i else None for j in range(SUB)] for i in range(SUB)]
        p = [spread(rows[b][r : r + 1, :]) for r in range(SUB)]
        x = [spread(inverse[b][r : r + 1, :]) for r in range(SUB)]
        below = range(b + 1, blocks)
        panel = {i: [spread(rows[i][:, base + r : base + r + 1]) for r in range(SUB)] for i in below}
        for k in range(0, SUB, 2):
            a, h, c = m[k][k], m[k + 1][k], m[k + 1][k + 1]
            by_first = refined(pl.reciprocal(a, approx=True), a)
            ratio = h * by_first
            d = c - h * ratio
            by_second = refined(a * pl.reciprocal(a * c - h * h, approx=True), d)
            p[k + 1] = p[k + 1] - ratio * p[k]
            x[k + 1] = x[k + 1] - ratio * x[k]
            put(base + k, x[k], a)
            put(base + k + 1, x[k + 1], d)
            f, t = {}, {}
            for i in range(k + 2, SUB):
                f0 = m[i][k] * by_first
                t[i] = m[i][k + 1] - f0 * h
                f[i] = (f0, t[i] * by_second)
            for j in range(k + 2, SUB):
                for i in range(j, SUB):
                    m[i][j] = (m[i][j] - f[i][0] * m[j][k]) - f[i][1] * t[j]
            for i in range(k + 2, SUB):
                p[i] = (p[i] - f[i][0] * p[k]) - f[i][1] * p[k + 1]
                x[i] = (x[i] - f[i][0] * x[k]) - f[i][1] * x[k + 1]
            for i in below:
                column = panel[i]
                f0 = column[k] * by_first
                f1 = (column[k + 1] - f0 * h) * by_second
                for j in range(k + 2, SUB):
                    column[j] = (column[j] - f0 * m[j][k]) - f1 * t[j]
                rows[i] = (rows[i] - f0 * p[k]) - f1 * p[k + 1]
                inverse[i] = (inverse[i] - f0 * x[k]) - f1 * x[k + 1]


def finish_kernel(total_rows, terms, update_ref, *refs):
    term_refs, out_ref, weight = refs[:terms], refs[terms], refs[terms + 1]
    summed = term_refs[0][...]
    for ref in term_refs[1:]:
        summed = summed + ref[...]
    row = lax.broadcasted_iota(jnp.int32, summed.shape, 0)
    column = lax.broadcasted_iota(jnp.int32, summed.shape, 1)
    gram = summed / total_rows + jnp.where(row == column, EPSILON, 0.0)

    def put(k, x, pivot):
        weight[k : k + 1, :] = (x * lax.rsqrt(pivot))[0:1, :]

    factor_inverse(gram, put)
    w_high, w_low = split(weight[...])
    across = (((1,), (1,)), ((), ()))
    dot = functools.partial(lax.dot_general, dimension_numbers=across, preferred_element_type=jnp.float32)
    for start in range(0, out_ref.shape[0], CHUNK):
        high, low = split(update_ref[start : start + CHUNK, :])
        out_ref[start : start + CHUNK, :] = dot(high, w_high) + dot(high, w_low) + dot(low, w_high)


def summed_over(x, axis):
    count = lax.axis_size(axis)
    if count & (count - 1):
        return [lax.psum(x, axis)]
    terms = [x]
    stride = 1
    while stride < count:
        total = functools.reduce(jnp.add, terms)
        terms = [total]
        for by in (1, 2, 3):
            if stride * by < count:
                terms.append(lax.ppermute(total, axis, [(i, i ^ (stride * by)) for i in range(count)]))
        stride *= 4
    return terms


def body(sketch, tile_values, sent_blocks, pair_counts):
    side_pos = lax.axis_index("side")
    owner = lax.axis_index("shard")
    owners = lax.axis_size("shard")
    own_sketch = sketch[0]
    tiles = tile_values[0]
    rows = own_sketch.shape[0]
    lists = lax.dynamic_index_in_dim(sent_blocks, side_pos, 0, keepdims=False)
    counts = lax.dynamic_index_in_dim(pair_counts, side_pos, 0, keepdims=False)
    plan = routes(owners)
    plan.append((list(range(owners)), [HALF] * owners, [HALF] * owners))
    pack_pairs = jnp.array([r[1] for r in plan], jnp.int32).T[owner]
    use_pairs = jnp.array([r[2] for r in plan], jnp.int32).T[owner]
    packed = pl.pallas_call(
        pack_kernel,
        out_shape=[pltpu.VMEM((EXTENT, RANK), jnp.bfloat16)] * len(plan),
        in_specs=[SMEM, SMEM, SMEM, VMEM],
        out_specs=[VMEM] * len(plan),
        compiler_params=pltpu.CompilerParams(vmem_limit_bytes=8 * MIB),
        name="pack_blocks",
    )(pack_pairs, lists, counts, own_sketch)
    arrived = []
    for (partner, _, _), block in zip(plan, packed):
        pairs = [
            (side * owners + o, (1 - side) * owners + partner[o]) for side in (0, 1) for o in range(owners)
        ]
        arrived.append(lax.ppermute(block, ("side", "shard"), pairs))
    update = None
    order = [len(plan) - 1] + list(range(len(plan) - 1))
    for position in order:
        first = update is None
        update = pl.pallas_call(
            functools.partial(first_kernel if first else next_kernel, position),
            out_shape=pltpu.VMEM((rows, RANK), jnp.float32),
            in_specs=[SMEM, SMEM, SMEM, ANY, VMEM] + ([] if first else [VMEM]),
            out_specs=VMEM,
            scratch_shapes=[
                pltpu.VMEM((EXTENT // CHUNK, CHUNK, EXTENT), jnp.bfloat16),
                pltpu.SemaphoreType.DMA((EXTENT // CHUNK,)),
            ],
            input_output_aliases={} if first else {5: 0},
            compiler_params=pltpu.CompilerParams(vmem_limit_bytes=8 * MIB),
            cost_estimate=pl.CostEstimate(
                flops=2 * EXTENT * EXTENT * RANK, bytes_accessed=2 * EXTENT * EXTENT, transcendentals=0
            ),
            name="add_pair_product",
        )(use_pairs, lists, counts, tiles, resident(arrived[position]), *([] if first else [update]))
    gram = pl.pallas_call(
        gram_kernel,
        out_shape=pltpu.VMEM((RANK, RANK), jnp.float32),
        in_specs=[VMEM],
        out_specs=VMEM,
        compiler_params=pltpu.CompilerParams(vmem_limit_bytes=8 * MIB),
        name="gram",
    )(resident(update))
    terms = summed_over(gram, "shard")
    result = pl.pallas_call(
        functools.partial(finish_kernel, float(rows * owners), len(terms)),
        out_shape=jax.ShapeDtypeStruct((rows, RANK), jnp.float32),
        in_specs=[VMEM] * (1 + len(terms)),
        out_specs=VMEM,
        scratch_shapes=[pltpu.VMEM((RANK, RANK), jnp.float32)],
        compiler_params=pltpu.CompilerParams(vmem_limit_bytes=8 * MIB),
        name="factor_and_apply",
    )(resident(update), *[resident(t) for t in terms])
    return result[None]


def solution(mesh):
    return jax.shard_map(
        body,
        mesh=mesh,
        in_specs=(
            P("side", "shard", None),
            P("side", "shard", None),
            P(None, "shard"),
            P(None, "shard"),
        ),
        out_specs=P("side", "shard", None),
        check_vma=False,
    )
```

```python
import functools
import jax
import jax.numpy as jnp
from jax import lax
from jax.experimental import pallas as pl
from jax.experimental.pallas import tpu as pltpu
from jax.sharding import PartitionSpec as P

TB = 128
RANK = 128
PEER = 8
HALF = 2
PAIRS = 5
EXTENT = PEER * TB
EPSILON = 1e-05
SUB = 8
CHUNK = 256
MIB = 1 << 20
GROUPS = ((4,),(0,),(1,),(3,2))
FIRST = (0,4)

VMEM = pl.BlockSpec(memory_space=pltpu.VMEM)
SMEM = pl.BlockSpec(memory_space=pltpu.SMEM)
ANY = pl.BlockSpec(memory_space=pl.ANY)


def resident(x):
    return pltpu.with_memory_space_constraint(x, pltpu.VMEM)


def routes(owners):
    if owners % 4 == 0:
        up = [
            lambda o: (o // 2) % 2 == 0,
            lambda o: o % 2 == 1,
            lambda o: (o // 2) % 2 == 1,
            lambda o: o % 2 == 0,
        ]
        reach = [2, 1, 2, 1]
        made = []
        for is_up, by in zip(up, reach):
            partner = [(o + (by if is_up(o) else -by)) % owners for o in range(owners)]
            pair = [HALF + (by if is_up(o) else -by) for o in range(owners)]
            made.append((partner, pair, pair))
        return made
    made = []
    for by in (2, 1, -2, -1):
        partner = [(o + by) % owners for o in range(owners)]
        made.append((partner, [HALF + by] * owners, [HALF - by] * owners))
    return made


def pair_position(table, owner):
    value = table[3]
    for place in (2, 1, 0):
        value = jnp.where(lax.rem(owner, 4) == place, table[place], value)
    return value


def pack(tables, lists, counts, sketch, out_refs):
    side = lax.axis_index("side")
    owner = lax.axis_index("shard")
    for table, out_ref in zip(tables, out_refs):
        pair = pair_position(table, owner)
        live = counts[side, pair]
        for slot in range(PEER):
            start = pl.multiple_of(lists[side, pair * PEER + slot] * TB, TB)
            block = sketch[pl.ds(start, TB), :]
            out_ref[slot * TB : (slot + 1) * TB, :] = jnp.where(slot < live, block, jnp.zeros_like(block))


def first_pack_kernel(tables, lists_ref, counts_ref, sketch_ref, lists, counts, held, *refs):
    out_refs, sems = refs[:-1], refs[-1]
    copies = [
        pltpu.make_async_copy(source, target, sems.at[i])
        for i, (source, target) in enumerate(((sketch_ref, held), (lists_ref, lists), (counts_ref, counts)))
    ]
    for copy in copies:
        copy.start()
    for copy in copies[::-1]:
        copy.wait()
    pack(tables, lists, counts, held, out_refs)


def second_pack_kernel(tables, lists, counts, held, *out_refs):
    pack(tables, lists, counts, held, out_refs)


def add_product(table, lists_ref, counts_ref, tile_ref, fetched_ref, update_ref):
    side = lax.axis_index("side")
    pair = pair_position(table, lax.axis_index("shard"))
    live = counts_ref[side, pair]
    unused = update_ref.shape[0] // TB - 1
    fetched = fetched_ref[...]
    for first in range(0, PEER, CHUNK // TB):
        start = pl.multiple_of(pair * EXTENT + first * TB, CHUNK)
        part = jnp.dot(tile_ref[pl.ds(start, CHUNK), :], fetched, preferred_element_type=jnp.float32)
        for step in range(CHUNK // TB):
            slot = first + step
            block = jnp.where(slot < live, lists_ref[side, pair * PEER + slot], unused)
            rows = pl.ds(pl.multiple_of(block * TB, TB), TB)
            update_ref[rows, :] += part[step * TB : (step + 1) * TB, :]


def first_kernel(tables, lists_ref, counts_ref, tile_ref, *refs):
    fetched_refs, update_ref = refs[: len(tables)], refs[len(tables)]
    update_ref[...] = jnp.zeros_like(update_ref)
    for table, fetched_ref in zip(tables, fetched_refs):
        add_product(table, lists_ref, counts_ref, tile_ref, fetched_ref, update_ref)


def next_kernel(tables, lists_ref, counts_ref, tile_ref, *refs):
    fetched_refs, (_, update_ref) = refs[: len(tables)], refs[len(tables) :]
    for table, fetched_ref in zip(tables, fetched_refs):
        add_product(table, lists_ref, counts_ref, tile_ref, fetched_ref, update_ref)


def last_kernel(tables, lists_ref, counts_ref, tile_ref, *refs):
    fetched_refs, (_, update_ref, gram_ref, high_ref, low_ref) = refs[: len(tables)], refs[len(tables) :]
    for table, fetched_ref in zip(tables, fetched_refs):
        add_product(table, lists_ref, counts_ref, tile_ref, fetched_ref, update_ref)
    high, low = split(update_ref[: high_ref.shape[0], :])
    high_ref[...] = high
    low_ref[...] = low
    down = (((0,), (0,)), ((), ()))
    dot = functools.partial(lax.dot_general, dimension_numbers=down, preferred_element_type=jnp.float32)
    gram_ref[...] = dot(high, high) + dot(high, low) + dot(low, high)


def split(x):
    high = x.astype(jnp.bfloat16)
    low = (x - high.astype(jnp.float32)).astype(jnp.bfloat16)
    return high, low


def refined(guess, value):
    for _ in range(2):
        guess = guess * (2.0 - value * guess)
    return guess


def factor_inverse(gram, put):
    width = gram.shape[1]
    blocks = width // SUB
    spread = lambda x: jnp.broadcast_to(x, (SUB, width))
    sub = lax.broadcasted_iota(jnp.int32, (SUB, width), 0)
    lane = lax.broadcasted_iota(jnp.int32, (SUB, width), 1)
    rows = [gram[i * SUB : (i + 1) * SUB, :] for i in range(blocks)]
    inverse = [jnp.where(lane == sub + i * SUB, 1.0, 0.0) for i in range(blocks)]
    for b in range(blocks):
        base = b * SUB
        columns = [spread(rows[b][:, base + r : base + r + 1]) for r in range(SUB)]
        m = [[spread(columns[j][i : i + 1, :]) if j <= i else None for j in range(SUB)] for i in range(SUB)]
        p = [spread(rows[b][r : r + 1, :]) for r in range(SUB)]
        x = [spread(inverse[b][r : r + 1, :]) for r in range(SUB)]
        below = range(b + 1, blocks)
        panel = {i: [spread(rows[i][:, base + r : base + r + 1]) for r in range(SUB)] for i in below}
        for k in range(0, SUB, 2):
            a, h, c = m[k][k], m[k + 1][k], m[k + 1][k + 1]
            by_first = refined(pl.reciprocal(a, approx=True), a)
            ratio = h * by_first
            d = c - h * ratio
            by_second = refined(a * pl.reciprocal(a * c - h * h, approx=True), d)
            p[k + 1] = p[k + 1] - ratio * p[k]
            x[k + 1] = x[k + 1] - ratio * x[k]
            put(base + k, x[k], a)
            put(base + k + 1, x[k + 1], d)
            f, t = {}, {}
            for i in range(k + 2, SUB):
                f0 = m[i][k] * by_first
                t[i] = m[i][k + 1] - f0 * h
                f[i] = (f0, t[i] * by_second)
            for j in range(k + 2, SUB):
                for i in range(j, SUB):
                    m[i][j] = (m[i][j] - f[i][0] * m[j][k]) - f[i][1] * t[j]
            for i in range(k + 2, SUB):
                p[i] = (p[i] - f[i][0] * p[k]) - f[i][1] * p[k + 1]
                x[i] = (x[i] - f[i][0] * x[k]) - f[i][1] * x[k + 1]
            for i in below:
                column = panel[i]
                f0 = column[k] * by_first
                f1 = (column[k + 1] - f0 * h) * by_second
                for j in range(k + 2, SUB):
                    column[j] = (column[j] - f0 * m[j][k]) - f1 * t[j]
                rows[i] = (rows[i] - f0 * p[k]) - f1 * p[k + 1]
                inverse[i] = (inverse[i] - f0 * x[k]) - f1 * x[k + 1]


def finish_kernel(total_rows, terms, high_ref, low_ref, *refs):
    term_refs, out_ref, weight, made, sems = refs[:terms], *refs[terms:]
    summed = term_refs[0][...]
    for ref in term_refs[1:]:
        summed = summed + ref[...]
    row = lax.broadcasted_iota(jnp.int32, summed.shape, 0)
    column = lax.broadcasted_iota(jnp.int32, summed.shape, 1)
    gram = summed / total_rows + jnp.where(row == column, EPSILON, 0.0)

    def put(k, x, pivot):
        weight[k : k + 1, :] = (x * lax.rsqrt(pivot))[0:1, :]

    factor_inverse(gram, put)
    w_high, w_low = split(weight[...])
    across = (((1,), (1,)), ((), ()))
    dot = functools.partial(lax.dot_general, dimension_numbers=across, preferred_element_type=jnp.float32)
    copies = []
    for part in range(made.shape[0]):
        rows = slice(part * made.shape[1], (part + 1) * made.shape[1])
        high, low = high_ref[rows, :], low_ref[rows, :]
        made[part] = dot(high, w_high) + dot(high, w_low) + dot(low, w_high)
        copy = pltpu.make_async_copy(made.at[part], out_ref.at[rows, :], sems.at[part])
        copy.start()
        copies.append(copy)
    for copy in copies:
        copy.wait()


def summed_over(x, axis):
    count = lax.axis_size(axis)
    if count & (count - 1):
        return [lax.psum(x, axis)]
    terms = [x]
    stride = 1
    while stride < count:
        total = functools.reduce(jnp.add, terms)
        terms = [total]
        for by in (1, 2, 3):
            if stride * by < count:
                terms.append(lax.ppermute(total, axis, [(i, i ^ (stride * by)) for i in range(count)]))
        stride *= 4
    return terms


def body(sketch, tile_values, sent_blocks, pair_counts):
    owners = lax.axis_size("shard")
    own_sketch = sketch[0]
    tiles = tile_values[0]
    rows = own_sketch.shape[0]
    plan = routes(owners)
    plan.append((list(range(owners)), [HALF] * owners, [HALF] * owners))
    block_shape = pltpu.VMEM((EXTENT, RANK), jnp.bfloat16)
    lists, counts, held, *packed = pl.pallas_call(
        functools.partial(first_pack_kernel, [plan[position][1][:4] for position in FIRST]),
        out_shape=[
            pltpu.SMEM(sent_blocks.shape, jnp.int32),
            pltpu.SMEM(pair_counts.shape, jnp.int32),
            pltpu.VMEM((rows, RANK), jnp.bfloat16),
        ]
        + [block_shape] * len(FIRST),
        in_specs=[ANY, ANY, ANY],
        out_specs=[SMEM, SMEM, VMEM] + [VMEM] * len(FIRST),
        scratch_shapes=[pltpu.SemaphoreType.DMA((3,))],
        compiler_params=pltpu.CompilerParams(vmem_limit_bytes=8 * MIB),
        name="pack_first",
    )(*[pltpu.with_memory_space_constraint(x, pltpu.HBM) for x in (sent_blocks, pair_counts, own_sketch)])
    second = [position for position in range(len(plan)) if position not in FIRST]
    lists, counts = [pltpu.with_memory_space_constraint(x, pltpu.SMEM) for x in (lists, counts)]
    if second:
        packed += pl.pallas_call(
            functools.partial(second_pack_kernel, [plan[position][1][:4] for position in second]),
            out_shape=[block_shape] * len(second),
            in_specs=[SMEM, SMEM, VMEM],
            out_specs=[VMEM] * len(second),
            compiler_params=pltpu.CompilerParams(vmem_limit_bytes=8 * MIB),
            name="pack_second",
        )(lists, counts, resident(held))
    packed = dict(zip(list(FIRST) + second, packed))
    packed = [packed[position] for position in range(len(plan))]
    arrived = []
    for (partner, _, _), block in zip(plan, packed):
        pairs = [
            (side * owners + o, (1 - side) * owners + partner[o]) for side in (0, 1) for o in range(owners)
        ]
        arrived.append(lax.ppermute(block, ("side", "shard"), pairs))
    update_shape = pltpu.VMEM((rows + TB, RANK), jnp.float32)
    half_shape = pltpu.VMEM((rows, RANK), jnp.bfloat16)
    tiles = resident(tiles)
    state = []
    groups = GROUPS
    for group in groups:
        last = group is groups[-1]
        kernel = last_kernel if last else next_kernel if state else first_kernel
        state = pl.pallas_call(
            functools.partial(kernel, [plan[position][2][:4] for position in group]),
            out_shape=[update_shape] + ([pltpu.VMEM((RANK, RANK), jnp.float32), half_shape, half_shape] if last else []),
            in_specs=[SMEM, SMEM, VMEM] + [VMEM] * (len(group) + len(state)),
            out_specs=[VMEM] * (4 if last else 1),
            input_output_aliases={3 + len(group): 0} if state else {},
            compiler_params=pltpu.CompilerParams(vmem_limit_bytes=8 * MIB),
            cost_estimate=pl.CostEstimate(
                flops=2 * EXTENT * EXTENT * RANK * len(group),
                bytes_accessed=2 * EXTENT * EXTENT * len(group),
                transcendentals=0,
            ),
            name="add_pair_products",
        )(
            lists,
            counts,
            tiles,
            *[resident(arrived[position]) for position in group],
            *[resident(x) for x in state],
        )
    _, gram, high, low = state
    terms = summed_over(gram, "shard")
    result = pl.pallas_call(
        functools.partial(finish_kernel, float(rows * owners), len(terms)),
        out_shape=jax.ShapeDtypeStruct((rows, RANK), jnp.float32),
        in_specs=[VMEM] * (2 + len(terms)),
        out_specs=ANY,
        scratch_shapes=[
            pltpu.VMEM((RANK, RANK), jnp.float32),
            pltpu.VMEM((rows // CHUNK, CHUNK, RANK), jnp.float32),
            pltpu.SemaphoreType.DMA((rows // CHUNK,)),
        ],
        compiler_params=pltpu.CompilerParams(vmem_limit_bytes=8 * MIB),
        name="factor_and_apply",
    )(resident(high), resident(low), *[resident(t) for t in terms])
    return result[None]


def solution(mesh):
    return jax.shard_map(
        body,
        mesh=mesh,
        in_specs=(
            P("side", "shard", None),
            P("side", "shard", None),
            P(None, "shard"),
            P(None, "shard"),
        ),
        out_specs=P("side", "shard", None),
        check_vma=False,
    )
```

```python
import functools
import jax
import jax.numpy as jnp
from jax import lax
from jax.experimental import pallas as pl
from jax.experimental.pallas import tpu as pltpu
from jax.sharding import PartitionSpec as P

TB = 128
RANK = 128
PEER = 8
HALF = 2
PAIRS = 5
EXTENT = PEER * TB
EPSILON = 1e-05
SUB = 8
CHUNK = 256
MIB = 1 << 20
GROUPS = ((4,),(0,),(1,),(3,2))
FIRST = (0,4)

VMEM = pl.BlockSpec(memory_space=pltpu.VMEM)
SMEM = pl.BlockSpec(memory_space=pltpu.SMEM)
ANY = pl.BlockSpec(memory_space=pl.ANY)


def resident(x):
    return pltpu.with_memory_space_constraint(x, pltpu.VMEM)


def routes(owners):
    if owners % 4 == 0:
        up = [
            lambda o: (o // 2) % 2 == 0,
            lambda o: o % 2 == 1,
            lambda o: (o // 2) % 2 == 1,
            lambda o: o % 2 == 0,
        ]
        reach = [2, 1, 2, 1]
        made = []
        for is_up, by in zip(up, reach):
            partner = [(o + (by if is_up(o) else -by)) % owners for o in range(owners)]
            pair = [HALF + (by if is_up(o) else -by) for o in range(owners)]
            made.append((partner, pair, pair))
        return made
    made = []
    for by in (2, 1, -2, -1):
        partner = [(o + by) % owners for o in range(owners)]
        made.append((partner, [HALF + by] * owners, [HALF - by] * owners))
    return made


def pair_position(table, owner):
    value = table[3]
    for place in (2, 1, 0):
        value = jnp.where(lax.rem(owner, 4) == place, table[place], value)
    return value


def pack(tables, lists, counts, sketch, out_refs):
    side = lax.axis_index("side")
    owner = lax.axis_index("shard")
    for table, out_ref in zip(tables, out_refs):
        pair = pair_position(table, owner)
        live = counts[side, pair]
        for slot in range(PEER):
            start = pl.multiple_of(lists[side, pair * PEER + slot] * TB, TB)
            block = sketch[pl.ds(start, TB), :]
            out_ref[slot * TB : (slot + 1) * TB, :] = jnp.where(slot < live, block, jnp.zeros_like(block))


def first_pack_kernel(tables, lists_ref, counts_ref, sketch_ref, lists, counts, held, *refs):
    out_refs, sems = refs[:-1], refs[-1]
    copies = [
        pltpu.make_async_copy(source, target, sems.at[i])
        for i, (source, target) in enumerate(((sketch_ref, held), (lists_ref, lists), (counts_ref, counts)))
    ]
    for copy in copies:
        copy.start()
    for copy in copies[::-1]:
        copy.wait()
    pack(tables, lists, counts, held, out_refs)


def second_pack_kernel(tables, lists, counts, held, *out_refs):
    pack(tables, lists, counts, held, out_refs)


def add_product(table, lists_ref, counts_ref, tile_ref, fetched_ref, update_ref):
    side = lax.axis_index("side")
    pair = pair_position(table, lax.axis_index("shard"))
    live = counts_ref[side, pair]
    unused = update_ref.shape[0] // TB - 1
    fetched = fetched_ref[...]
    for first in range(0, PEER, CHUNK // TB):
        start = pl.multiple_of(pair * EXTENT + first * TB, CHUNK)
        part = jnp.dot(tile_ref[pl.ds(start, CHUNK), :], fetched, preferred_element_type=jnp.float32)
        for step in range(CHUNK // TB):
            slot = first + step
            block = jnp.where(slot < live, lists_ref[side, pair * PEER + slot], unused)
            rows = pl.ds(pl.multiple_of(block * TB, TB), TB)
            update_ref[rows, :] += part[step * TB : (step + 1) * TB, :]


def first_kernel(tables, lists_ref, counts_ref, tile_ref, *refs):
    fetched_refs, update_ref = refs[: len(tables)], refs[len(tables)]
    update_ref[...] = jnp.zeros_like(update_ref)
    for table, fetched_ref in zip(tables, fetched_refs):
        add_product(table, lists_ref, counts_ref, tile_ref, fetched_ref, update_ref)


def next_kernel(tables, lists_ref, counts_ref, tile_ref, *refs):
    fetched_refs, (_, update_ref) = refs[: len(tables)], refs[len(tables) :]
    for table, fetched_ref in zip(tables, fetched_refs):
        add_product(table, lists_ref, counts_ref, tile_ref, fetched_ref, update_ref)


def last_kernel(tables, lists_ref, counts_ref, tile_ref, *refs):
    fetched_refs, (_, update_ref, fold_ref, halves_ref) = refs[: len(tables)], refs[len(tables) :]
    for table, fetched_ref in zip(tables, fetched_refs):
        add_product(table, lists_ref, counts_ref, tile_ref, fetched_ref, update_ref)
    rows, width = halves_ref.shape[0], halves_ref.shape[1] // 2
    high, low = split(update_ref[:rows, :])
    halves_ref[:, :width] = high
    halves_ref[:, width:] = low
    both = lax.dot_general(
        high, halves_ref[...], (((0,), (0,)), ((), ())), preferred_element_type=jnp.float32
    )
    mixed = both[:, width:]
    fold_ref[...] = folded(both[:, :width] + mixed + mixed.T)


def grid_of(shape):
    return lax.broadcasted_iota(jnp.int32, shape, 0), lax.broadcasted_iota(jnp.int32, shape, 1)


def folded(gram):
    half = gram.shape[0] // 2
    top, bottom = gram[:half, :], gram[half:, :]
    row, column = grid_of(top.shape)
    turned = pltpu.roll(bottom, half, 1)
    main = jnp.where((column < half) & (row > column), turned, top)
    corner = jnp.sum(jnp.where(column - half == row, bottom, 0.0), axis=0, keepdims=True)
    return jnp.concatenate([main, jnp.broadcast_to(corner, (SUB, gram.shape[1]))], axis=0)


def unfolded(fold):
    half = fold.shape[1] // 2
    main = fold[:half, :]
    row, column = grid_of(main.shape)
    across = jnp.concatenate([main, jnp.zeros_like(main)], axis=0).T
    mirror = across[:half, :]
    left = column < half
    top = jnp.where(left & (row > column), mirror, main)
    turned = pltpu.roll(jnp.where(row > column, main, mirror), half, 1)
    corner = jnp.broadcast_to(fold[half : half + 1, :], main.shape)
    bottom = jnp.where(left, across[half:, :], jnp.where(column - half == row, corner, turned))
    return jnp.concatenate([top, bottom], axis=0)


def split(x):
    high = x.astype(jnp.bfloat16)
    low = (x - high.astype(jnp.float32)).astype(jnp.bfloat16)
    return high, low


def refined(guess, value):
    return guess * (2.0 - value * guess)


def factor_inverse(gram, put):
    width = gram.shape[1]
    blocks = width // SUB
    spread = lambda x: jnp.broadcast_to(x, (SUB, width))
    row, lane = grid_of((SUB, width))
    rows = [gram[i * SUB : (i + 1) * SUB, :] for i in range(blocks)]
    for b in range(blocks):
        base = b * SUB
        here = (lane >= base) & (lane < base + SUB)
        done = lane < base + SUB
        columns = [spread(rows[b][:, base + r : base + r + 1]) for r in range(SUB)]
        m = [[spread(columns[j][i : i + 1, :]) if j <= i else None for j in range(SUB)] for i in range(SUB)]
        own = jnp.where(here, jnp.where(lane == base + row, 1.0, 0.0), rows[b])
        p = [spread(own[r : r + 1, :]) for r in range(SUB)]
        below = range(b + 1, blocks)
        panel = {i: [spread(rows[i][:, base + r : base + r + 1]) for r in range(SUB)] for i in below}
        for i in below:
            rows[i] = jnp.where(here, 0.0, rows[i])
        for k in range(0, SUB, 2):
            a, h, c = m[k][k], m[k + 1][k], m[k + 1][k + 1]
            by_first = refined(pl.reciprocal(a, approx=True), a)
            ratio = h * by_first
            d = c - h * ratio
            by_second = refined(a * pl.reciprocal(a * c - h * h, approx=True), d)
            p[k + 1] = p[k + 1] - ratio * p[k]
            put(base + k, jnp.where(done, p[k], 0.0), a)
            put(base + k + 1, jnp.where(done, p[k + 1], 0.0), d)
            f, t = {}, {}
            for i in range(k + 2, SUB):
                f0 = m[i][k] * by_first
                t[i] = m[i][k + 1] - f0 * h
                f[i] = (f0, t[i] * by_second)
            for j in range(k + 2, SUB):
                for i in range(j, SUB):
                    m[i][j] = (m[i][j] - f[i][0] * m[j][k]) - f[i][1] * t[j]
            for i in range(k + 2, SUB):
                p[i] = (p[i] - f[i][0] * p[k]) - f[i][1] * p[k + 1]
            for i in below:
                column = panel[i]
                f0 = column[k] * by_first
                f1 = (column[k + 1] - f0 * h) * by_second
                for j in range(k + 2, SUB):
                    column[j] = (column[j] - f0 * m[j][k]) - f1 * t[j]
                rows[i] = (rows[i] - f0 * p[k]) - f1 * p[k + 1]


def finish_kernel(total_rows, terms, halves_ref, *refs):
    term_refs, out_ref, weight, made, sems = refs[:terms], *refs[terms:]
    summed = term_refs[0][...]
    for ref in term_refs[1:]:
        summed = summed + ref[...]
    width = summed.shape[1]
    row, column = grid_of((width, width))
    gram = unfolded(summed) / total_rows + jnp.where(row == column, EPSILON, 0.0)

    def put(k, x, pivot):
        weight[k : k + 1, :] = (x * lax.rsqrt(pivot))[0:1, :]

    factor_inverse(gram, put)
    high, low = split(weight[...])
    both = jnp.concatenate(
        [jnp.concatenate([high, high], axis=1), jnp.concatenate([low, jnp.zeros_like(low)], axis=1)], axis=0
    )
    copies = []
    for part in range(made.shape[0]):
        rows = slice(part * made.shape[1], (part + 1) * made.shape[1])
        product = lax.dot_general(
            halves_ref[rows, :], both, (((1,), (1,)), ((), ())), preferred_element_type=jnp.float32
        )
        made[part] = product[:, :width] + product[:, width:]
        copy = pltpu.make_async_copy(made.at[part], out_ref.at[rows, :], sems.at[part])
        copy.start()
        copies.append(copy)
    for copy in copies:
        copy.wait()


def summed_over(x, axis):
    count = lax.axis_size(axis)
    if count & (count - 1):
        return [lax.psum(x, axis)]
    terms = [x]
    stride = 1
    while stride < count:
        total = functools.reduce(jnp.add, terms)
        terms = [total]
        for by in (1, 2, 3):
            if stride * by < count:
                terms.append(lax.ppermute(total, axis, [(i, i ^ (stride * by)) for i in range(count)]))
        stride *= 4
    return terms


def body(sketch, tile_values, sent_blocks, pair_counts):
    owners = lax.axis_size("shard")
    own_sketch = sketch[0]
    tiles = tile_values[0]
    rows = own_sketch.shape[0]
    plan = routes(owners)
    plan.append((list(range(owners)), [HALF] * owners, [HALF] * owners))
    block_shape = pltpu.VMEM((EXTENT, RANK), jnp.bfloat16)
    lists, counts, held, *packed = pl.pallas_call(
        functools.partial(first_pack_kernel, [plan[position][1][:4] for position in FIRST]),
        out_shape=[
            pltpu.SMEM(sent_blocks.shape, jnp.int32),
            pltpu.SMEM(pair_counts.shape, jnp.int32),
            pltpu.VMEM((rows, RANK), jnp.bfloat16),
        ]
        + [block_shape] * len(FIRST),
        in_specs=[ANY, ANY, ANY],
        out_specs=[SMEM, SMEM, VMEM] + [VMEM] * len(FIRST),
        scratch_shapes=[pltpu.SemaphoreType.DMA((3,))],
        compiler_params=pltpu.CompilerParams(vmem_limit_bytes=8 * MIB),
        name="pack_first",
    )(*[pltpu.with_memory_space_constraint(x, pltpu.HBM) for x in (sent_blocks, pair_counts, own_sketch)])
    second = [position for position in range(len(plan)) if position not in FIRST]
    lists, counts = [pltpu.with_memory_space_constraint(x, pltpu.SMEM) for x in (lists, counts)]
    if second:
        packed += pl.pallas_call(
            functools.partial(second_pack_kernel, [plan[position][1][:4] for position in second]),
            out_shape=[block_shape] * len(second),
            in_specs=[SMEM, SMEM, VMEM],
            out_specs=[VMEM] * len(second),
            compiler_params=pltpu.CompilerParams(vmem_limit_bytes=8 * MIB),
            name="pack_second",
        )(lists, counts, resident(held))
    packed = dict(zip(list(FIRST) + second, packed))
    packed = [packed[position] for position in range(len(plan))]
    arrived = []
    for (partner, _, _), block in zip(plan, packed):
        pairs = [
            (side * owners + o, (1 - side) * owners + partner[o]) for side in (0, 1) for o in range(owners)
        ]
        arrived.append(lax.ppermute(block, ("side", "shard"), pairs))
    update_shape = pltpu.VMEM((rows + TB, RANK), jnp.float32)
    halves_shape = pltpu.VMEM((rows, 2 * RANK), jnp.bfloat16)
    fold_shape = pltpu.VMEM((RANK // 2 + SUB, RANK), jnp.float32)
    tiles = resident(tiles)
    state = []
    groups = GROUPS
    for group in groups:
        last = group is groups[-1]
        kernel = last_kernel if last else next_kernel if state else first_kernel
        state = pl.pallas_call(
            functools.partial(kernel, [plan[position][2][:4] for position in group]),
            out_shape=[update_shape] + ([fold_shape, halves_shape] if last else []),
            in_specs=[SMEM, SMEM, VMEM] + [VMEM] * (len(group) + len(state)),
            out_specs=[VMEM] * (3 if last else 1),
            input_output_aliases={3 + len(group): 0} if state else {},
            compiler_params=pltpu.CompilerParams(vmem_limit_bytes=8 * MIB),
            cost_estimate=pl.CostEstimate(
                flops=2 * EXTENT * EXTENT * RANK * len(group),
                bytes_accessed=2 * EXTENT * EXTENT * len(group),
                transcendentals=0,
            ),
            name="add_pair_products",
        )(
            lists,
            counts,
            tiles,
            *[resident(arrived[position]) for position in group],
            *[resident(x) for x in state],
        )
    _, fold, halves = state
    terms = summed_over(fold, "shard")
    result = pl.pallas_call(
        functools.partial(finish_kernel, float(rows * owners), len(terms)),
        out_shape=jax.ShapeDtypeStruct((rows, RANK), jnp.float32),
        in_specs=[VMEM] * (1 + len(terms)),
        out_specs=ANY,
        scratch_shapes=[
            pltpu.VMEM((RANK, RANK), jnp.float32),
            pltpu.VMEM((rows // CHUNK, CHUNK, RANK), jnp.float32),
            pltpu.SemaphoreType.DMA((rows // CHUNK,)),
        ],
        compiler_params=pltpu.CompilerParams(vmem_limit_bytes=8 * MIB),
        name="factor_and_apply",
    )(resident(halves), *[resident(t) for t in terms])
    return result[None]


def solution(mesh):
    return jax.shard_map(
        body,
        mesh=mesh,
        in_specs=(
            P("side", "shard", None),
            P("side", "shard", None),
            P(None, "shard"),
            P(None, "shard"),
        ),
        out_specs=P("side", "shard", None),
        check_vma=False,
    )
```

```python
import functools
import jax
import jax.numpy as jnp
from jax import lax
from jax.experimental import pallas as pl
from jax.experimental.pallas import tpu as pltpu
from jax.sharding import PartitionSpec as P

TB = 128
RANK = 128
PEER = 8
HALF = 2
PAIRS = 5
EXTENT = PEER * TB
EPSILON = 1e-05
SUB = 8
CHUNK = 256
MIB = 1 << 20
GROUPS = ((4,),(0,),(1,),(3,2))
FIRST = (0,4)

VMEM = pl.BlockSpec(memory_space=pltpu.VMEM)
SMEM = pl.BlockSpec(memory_space=pltpu.SMEM)
ANY = pl.BlockSpec(memory_space=pl.ANY)


def resident(x):
    return pltpu.with_memory_space_constraint(x, pltpu.VMEM)


def routes(owners):
    if owners % 4 == 0:
        up = [
            lambda o: (o // 2) % 2 == 0,
            lambda o: o % 2 == 1,
            lambda o: (o // 2) % 2 == 1,
            lambda o: o % 2 == 0,
        ]
        reach = [2, 1, 2, 1]
        made = []
        for is_up, by in zip(up, reach):
            partner = [(o + (by if is_up(o) else -by)) % owners for o in range(owners)]
            pair = [HALF + (by if is_up(o) else -by) for o in range(owners)]
            made.append((partner, pair, pair))
        return made
    made = []
    for by in (2, 1, -2, -1):
        partner = [(o + by) % owners for o in range(owners)]
        made.append((partner, [HALF + by] * owners, [HALF - by] * owners))
    return made


def pair_position(table, owner):
    value = table[3]
    for place in (2, 1, 0):
        value = jnp.where(lax.rem(owner, 4) == place, table[place], value)
    return value


def pack(tables, lists, counts, sketch, out_refs):
    side = lax.axis_index("side")
    owner = lax.axis_index("shard")
    for table, out_ref in zip(tables, out_refs):
        pair = pair_position(table, owner)
        live = counts[side, pair]
        for slot in range(PEER):
            start = pl.multiple_of(lists[side, pair * PEER + slot] * TB, TB)
            block = sketch[pl.ds(start, TB), :]
            out_ref[slot * TB : (slot + 1) * TB, :] = jnp.where(slot < live, block, jnp.zeros_like(block))


def first_pack_kernel(tables, lists_ref, counts_ref, sketch_ref, lists, counts, held, *refs):
    out_refs, sems = refs[:-1], refs[-1]
    copies = [
        pltpu.make_async_copy(source, target, sems.at[i])
        for i, (source, target) in enumerate(((sketch_ref, held), (lists_ref, lists), (counts_ref, counts)))
    ]
    for copy in copies:
        copy.start()
    for copy in copies[::-1]:
        copy.wait()
    pack(tables, lists, counts, held, out_refs)


def second_pack_kernel(tables, lists, counts, held, *out_refs):
    pack(tables, lists, counts, held, out_refs)


def add_product(table, lists_ref, counts_ref, tile_ref, fetched_ref, update_ref):
    side = lax.axis_index("side")
    pair = pair_position(table, lax.axis_index("shard"))
    live = counts_ref[side, pair]
    unused = update_ref.shape[0] // TB - 1
    fetched = fetched_ref[...]
    for first in range(0, PEER, CHUNK // TB):
        start = pl.multiple_of(pair * EXTENT + first * TB, CHUNK)
        part = jnp.dot(tile_ref[pl.ds(start, CHUNK), :], fetched, preferred_element_type=jnp.float32)
        for step in range(CHUNK // TB):
            slot = first + step
            block = jnp.where(slot < live, lists_ref[side, pair * PEER + slot], unused)
            rows = pl.ds(pl.multiple_of(block * TB, TB), TB)
            update_ref[rows, :] += part[step * TB : (step + 1) * TB, :]


def first_kernel(tables, lists_ref, counts_ref, tile_ref, *refs):
    fetched_refs, update_ref = refs[: len(tables)], refs[len(tables)]
    update_ref[...] = jnp.zeros_like(update_ref)
    for table, fetched_ref in zip(tables, fetched_refs):
        add_product(table, lists_ref, counts_ref, tile_ref, fetched_ref, update_ref)


def next_kernel(tables, lists_ref, counts_ref, tile_ref, *refs):
    fetched_refs, (_, update_ref) = refs[: len(tables)], refs[len(tables) :]
    for table, fetched_ref in zip(tables, fetched_refs):
        add_product(table, lists_ref, counts_ref, tile_ref, fetched_ref, update_ref)


def last_kernel(tables, lists_ref, counts_ref, tile_ref, *refs):
    fetched_refs, (_, update_ref, fold_ref, halves_ref) = refs[: len(tables)], refs[len(tables) :]
    for table, fetched_ref in zip(tables, fetched_refs):
        add_product(table, lists_ref, counts_ref, tile_ref, fetched_ref, update_ref)
    rows, width = halves_ref.shape[0], halves_ref.shape[1] // 2
    high, low = split(update_ref[:rows, :])
    halves_ref[:, :width] = high
    halves_ref[:, width:] = low
    both = lax.dot_general(
        high, halves_ref[...], (((0,), (0,)), ((), ())), preferred_element_type=jnp.float32
    )
    mixed = both[:, width:]
    fold_ref[...] = folded(both[:, :width] + mixed + mixed.T)


def grid_of(shape):
    return lax.broadcasted_iota(jnp.int32, shape, 0), lax.broadcasted_iota(jnp.int32, shape, 1)


def folded(gram):
    half = gram.shape[0] // 2
    top, bottom = gram[:half, :], gram[half:, :]
    row, column = grid_of(top.shape)
    turned = pltpu.roll(bottom, half, 1)
    main = jnp.where((column < half) & (row > column), turned, top)
    corner = jnp.sum(jnp.where(column - half == row, bottom, 0.0), axis=0, keepdims=True)
    return jnp.concatenate([main, jnp.broadcast_to(corner, (SUB, gram.shape[1]))], axis=0)


def unfolded(fold):
    half = fold.shape[1] // 2
    main = fold[:half, :]
    row, column = grid_of(main.shape)
    across = jnp.concatenate([main, jnp.zeros_like(main)], axis=0).T
    mirror = across[:half, :]
    left = column < half
    top = jnp.where(left & (row > column), mirror, main)
    turned = pltpu.roll(jnp.where(row > column, main, mirror), half, 1)
    corner = jnp.broadcast_to(fold[half : half + 1, :], main.shape)
    bottom = jnp.where(left, across[half:, :], jnp.where(column - half == row, corner, turned))
    return jnp.concatenate([top, bottom], axis=0)


def split(x):
    high = x.astype(jnp.bfloat16)
    low = (x - high.astype(jnp.float32)).astype(jnp.bfloat16)
    return high, low


def refined(guess, value):
    return guess * (2.0 - value * guess)


def factor_inverse(gram, stage, put):
    width = gram.shape[1]
    blocks = width // SUB
    spread = lambda x: jnp.broadcast_to(x, (SUB, width))
    row, lane = grid_of((SUB, width))
    rows = [gram[i * SUB : (i + 1) * SUB, :] for i in range(blocks)]
    for b in range(blocks):
        base = b * SUB
        here = (lane >= base) & (lane < base + SUB)
        done = lane < base + SUB
        columns = [spread(rows[b][:, base + r : base + r + 1]) for r in range(SUB)]
        for j, column in enumerate(columns):
            stage[b % 2, j] = column
        m = [[spread(stage[b % 2, j, i : i + 1, :]) if j <= i else None for j in range(SUB)] for i in range(SUB)]
        own = jnp.where(here, jnp.where(lane == base + row, 1.0, 0.0), rows[b])
        p = [spread(own[r : r + 1, :]) for r in range(SUB)]
        below = range(b + 1, blocks)
        panel = {i: [spread(rows[i][:, base + r : base + r + 1]) for r in range(SUB)] for i in below}
        for i in below:
            rows[i] = jnp.where(here, 0.0, rows[i])
        for k in range(0, SUB, 2):
            a, h, c = m[k][k], m[k + 1][k], m[k + 1][k + 1]
            by_first = refined(pl.reciprocal(a, approx=True), a)
            ratio = h * by_first
            det = a * c - h * h
            d = det * by_first
            by_second = a * refined(pl.reciprocal(det, approx=True), det)
            p[k + 1] = p[k + 1] - ratio * p[k]
            put(base + k, jnp.where(done, p[k], 0.0), a)
            put(base + k + 1, jnp.where(done, p[k + 1], 0.0), d)
            f, t = {}, {}
            for i in range(k + 2, SUB):
                f0 = m[i][k] * by_first
                t[i] = m[i][k + 1] - f0 * h
                f[i] = (f0, t[i] * by_second)
            for j in range(k + 2, SUB):
                for i in range(j, SUB):
                    m[i][j] = (m[i][j] - f[i][0] * m[j][k]) - f[i][1] * t[j]
            for i in range(k + 2, SUB):
                p[i] = (p[i] - f[i][0] * p[k]) - f[i][1] * p[k + 1]
            for i in below:
                column = panel[i]
                f0 = column[k] * by_first
                f1 = (column[k + 1] - f0 * h) * by_second
                for j in range(k + 2, SUB):
                    column[j] = (column[j] - f0 * m[j][k]) - f1 * t[j]
                rows[i] = (rows[i] - f0 * p[k]) - f1 * p[k + 1]


def finish_kernel(total_rows, terms, halves_ref, *refs):
    term_refs, out_ref, weight, stage, made, sems = refs[:terms], *refs[terms:]
    summed = term_refs[0][...]
    for ref in term_refs[1:]:
        summed = summed + ref[...]
    width = summed.shape[1]
    row, column = grid_of((width, width))
    gram = unfolded(summed) * (1.0 / total_rows) + jnp.where(row == column, EPSILON, 0.0)

    def put(k, x, pivot):
        weight[k : k + 1, :] = (x * lax.rsqrt(pivot))[0:1, :]

    factor_inverse(gram, stage, put)
    high, low = split(weight[...])
    both = jnp.concatenate(
        [jnp.concatenate([high, high], axis=1), jnp.concatenate([low, jnp.zeros_like(low)], axis=1)], axis=0
    )
    copies = []
    for part in range(made.shape[0]):
        rows = slice(part * made.shape[1], (part + 1) * made.shape[1])
        product = lax.dot_general(
            halves_ref[rows, :], both, (((1,), (1,)), ((), ())), preferred_element_type=jnp.float32
        )
        made[part] = product[:, :width] + product[:, width:]
        copy = pltpu.make_async_copy(made.at[part], out_ref.at[rows, :], sems.at[part])
        copy.start()
        copies.append(copy)
    for copy in copies:
        copy.wait()


def summed_over(x, axis):
    count = lax.axis_size(axis)
    if count & (count - 1):
        return [lax.psum(x, axis)]
    terms = [x]
    stride = 1
    while stride < count:
        total = functools.reduce(jnp.add, terms)
        terms = [total]
        for by in (1, 2, 3):
            if stride * by < count:
                terms.append(lax.ppermute(total, axis, [(i, i ^ (stride * by)) for i in range(count)]))
        stride *= 4
    return terms


def body(sketch, tile_values, sent_blocks, pair_counts):
    owners = lax.axis_size("shard")
    own_sketch = sketch[0]
    tiles = tile_values[0]
    rows = own_sketch.shape[0]
    plan = routes(owners)
    plan.append((list(range(owners)), [HALF] * owners, [HALF] * owners))
    block_shape = pltpu.VMEM((EXTENT, RANK), jnp.bfloat16)
    lists, counts, held, *packed = pl.pallas_call(
        functools.partial(first_pack_kernel, [plan[position][1][:4] for position in FIRST]),
        out_shape=[
            pltpu.SMEM(sent_blocks.shape, jnp.int32),
            pltpu.SMEM(pair_counts.shape, jnp.int32),
            pltpu.VMEM((rows, RANK), jnp.bfloat16),
        ]
        + [block_shape] * len(FIRST),
        in_specs=[ANY, ANY, ANY],
        out_specs=[SMEM, SMEM, VMEM] + [VMEM] * len(FIRST),
        scratch_shapes=[pltpu.SemaphoreType.DMA((3,))],
        compiler_params=pltpu.CompilerParams(vmem_limit_bytes=8 * MIB),
        name="pack_first",
    )(*[pltpu.with_memory_space_constraint(x, pltpu.HBM) for x in (sent_blocks, pair_counts, own_sketch)])
    second = [position for position in range(len(plan)) if position not in FIRST]
    lists, counts = [pltpu.with_memory_space_constraint(x, pltpu.SMEM) for x in (lists, counts)]
    if second:
        packed += pl.pallas_call(
            functools.partial(second_pack_kernel, [plan[position][1][:4] for position in second]),
            out_shape=[block_shape] * len(second),
            in_specs=[SMEM, SMEM, VMEM],
            out_specs=[VMEM] * len(second),
            compiler_params=pltpu.CompilerParams(vmem_limit_bytes=8 * MIB),
            name="pack_second",
        )(lists, counts, resident(held))
    packed = dict(zip(list(FIRST) + second, packed))
    packed = [packed[position] for position in range(len(plan))]
    arrived = []
    for (partner, _, _), block in zip(plan, packed):
        pairs = [
            (side * owners + o, (1 - side) * owners + partner[o]) for side in (0, 1) for o in range(owners)
        ]
        arrived.append(lax.ppermute(block, ("side", "shard"), pairs))
    update_shape = pltpu.VMEM((rows + TB, RANK), jnp.float32)
    halves_shape = pltpu.VMEM((rows, 2 * RANK), jnp.bfloat16)
    fold_shape = pltpu.VMEM((RANK // 2 + SUB, RANK), jnp.float32)
    tiles = resident(tiles)
    state = []
    groups = GROUPS
    for group in groups:
        last = group is groups[-1]
        kernel = last_kernel if last else next_kernel if state else first_kernel
        state = pl.pallas_call(
            functools.partial(kernel, [plan[position][2][:4] for position in group]),
            out_shape=[update_shape] + ([fold_shape, halves_shape] if last else []),
            in_specs=[SMEM, SMEM, VMEM] + [VMEM] * (len(group) + len(state)),
            out_specs=[VMEM] * (3 if last else 1),
            input_output_aliases={3 + len(group): 0} if state else {},
            compiler_params=pltpu.CompilerParams(vmem_limit_bytes=8 * MIB),
            cost_estimate=pl.CostEstimate(
                flops=2 * EXTENT * EXTENT * RANK * len(group),
                bytes_accessed=2 * EXTENT * EXTENT * len(group),
                transcendentals=0,
            ),
            name="add_pair_products",
        )(
            lists,
            counts,
            tiles,
            *[resident(arrived[position]) for position in group],
            *[resident(x) for x in state],
        )
    _, fold, halves = state
    terms = summed_over(fold, "shard")
    result = pl.pallas_call(
        functools.partial(finish_kernel, float(rows * owners), len(terms)),
        out_shape=jax.ShapeDtypeStruct((rows, RANK), jnp.float32),
        in_specs=[VMEM] * (1 + len(terms)),
        out_specs=ANY,
        scratch_shapes=[
            pltpu.VMEM((RANK, RANK), jnp.float32),
            pltpu.VMEM((2, SUB, SUB, RANK), jnp.float32),
            pltpu.VMEM((rows // CHUNK, CHUNK, RANK), jnp.float32),
            pltpu.SemaphoreType.DMA((rows // CHUNK,)),
        ],
        compiler_params=pltpu.CompilerParams(vmem_limit_bytes=8 * MIB),
        name="factor_and_apply",
    )(resident(halves), *[resident(t) for t in terms])
    return result[None]


def solution(mesh):
    return jax.shard_map(
        body,
        mesh=mesh,
        in_specs=(
            P("side", "shard", None),
            P("side", "shard", None),
            P(None, "shard"),
            P(None, "shard"),
        ),
        out_specs=P("side", "shard", None),
        check_vma=False,
    )
```

```python
import functools
import jax
import jax.numpy as jnp
from jax import lax
from jax.experimental import pallas as pl
from jax.experimental.pallas import tpu as pltpu
from jax.sharding import PartitionSpec as P

TB = 128
RANK = 128
PEER = 8
HALF = 2
PAIRS = 5
EXTENT = PEER * TB
EPSILON = 1e-05
SUB = 8
CHUNK = 256
MIB = 1 << 20
GROUPS = ((4,),(0,),(1,),(3,2))
FIRST = (0,4)

VMEM = pl.BlockSpec(memory_space=pltpu.VMEM)
SMEM = pl.BlockSpec(memory_space=pltpu.SMEM)
ANY = pl.BlockSpec(memory_space=pl.ANY)


def resident(x):
    return pltpu.with_memory_space_constraint(x, pltpu.VMEM)


def routes(owners):
    if owners % 4 == 0:
        up = [
            lambda o: (o // 2) % 2 == 0,
            lambda o: o % 2 == 1,
            lambda o: (o // 2) % 2 == 1,
            lambda o: o % 2 == 0,
        ]
        reach = [2, 1, 2, 1]
        made = []
        for is_up, by in zip(up, reach):
            partner = [(o + (by if is_up(o) else -by)) % owners for o in range(owners)]
            pair = [HALF + (by if is_up(o) else -by) for o in range(owners)]
            made.append((partner, pair, pair))
        return made
    made = []
    for by in (2, 1, -2, -1):
        partner = [(o + by) % owners for o in range(owners)]
        made.append((partner, [HALF + by] * owners, [HALF - by] * owners))
    return made


def pair_position(table, owner):
    value = table[3]
    for place in (2, 1, 0):
        value = jnp.where(lax.rem(owner, 4) == place, table[place], value)
    return value


def pack(tables, lists, counts, sketch, out_refs):
    side = lax.axis_index("side")
    owner = lax.axis_index("shard")
    for table, out_ref in zip(tables, out_refs):
        pair = pair_position(table, owner)
        live = counts[side, pair]
        for slot in range(PEER):
            start = pl.multiple_of(lists[side, pair * PEER + slot] * TB, TB)
            block = sketch[pl.ds(start, TB), :]
            out_ref[slot * TB : (slot + 1) * TB, :] = jnp.where(slot < live, block, jnp.zeros_like(block))


def first_pack_kernel(tables, lists_ref, counts_ref, sketch_ref, lists, counts, held, *refs):
    out_refs, sems = refs[:-1], refs[-1]
    copies = [
        pltpu.make_async_copy(source, target, sems.at[i])
        for i, (source, target) in enumerate(((sketch_ref, held), (lists_ref, lists), (counts_ref, counts)))
    ]
    for copy in copies:
        copy.start()
    for copy in copies[::-1]:
        copy.wait()
    pack(tables, lists, counts, held, out_refs)


def second_pack_kernel(tables, lists, counts, held, *out_refs):
    pack(tables, lists, counts, held, out_refs)


def add_product(table, lists_ref, counts_ref, tile_ref, fetched_ref, update_ref):
    side = lax.axis_index("side")
    pair = pair_position(table, lax.axis_index("shard"))
    live = counts_ref[side, pair]
    unused = update_ref.shape[0] // TB - 1
    fetched = fetched_ref[...]
    for first in range(0, PEER, CHUNK // TB):
        start = pl.multiple_of(pair * EXTENT + first * TB, CHUNK)
        part = jnp.dot(tile_ref[pl.ds(start, CHUNK), :], fetched, preferred_element_type=jnp.float32)
        for step in range(CHUNK // TB):
            slot = first + step
            block = jnp.where(slot < live, lists_ref[side, pair * PEER + slot], unused)
            rows = pl.ds(pl.multiple_of(block * TB, TB), TB)
            update_ref[rows, :] += part[step * TB : (step + 1) * TB, :]


def first_kernel(tables, lists_ref, counts_ref, tile_ref, *refs):
    fetched_refs, update_ref = refs[: len(tables)], refs[len(tables)]
    update_ref[...] = jnp.zeros_like(update_ref)
    for table, fetched_ref in zip(tables, fetched_refs):
        add_product(table, lists_ref, counts_ref, tile_ref, fetched_ref, update_ref)


def next_kernel(tables, lists_ref, counts_ref, tile_ref, *refs):
    fetched_refs, (_, update_ref) = refs[: len(tables)], refs[len(tables) :]
    for table, fetched_ref in zip(tables, fetched_refs):
        add_product(table, lists_ref, counts_ref, tile_ref, fetched_ref, update_ref)


def last_kernel(tables, lists_ref, counts_ref, tile_ref, *refs):
    fetched_refs, (_, update_ref, fold_ref, halves_ref) = refs[: len(tables)], refs[len(tables) :]
    for table, fetched_ref in zip(tables, fetched_refs):
        add_product(table, lists_ref, counts_ref, tile_ref, fetched_ref, update_ref)
    rows, width = halves_ref.shape[0], halves_ref.shape[1] // 2
    high, low = split(update_ref[:rows, :])
    halves_ref[:, :width] = high
    halves_ref[:, width:] = low
    both = lax.dot_general(
        high, halves_ref[...], (((0,), (0,)), ((), ())), preferred_element_type=jnp.float32
    )
    mixed = both[:, width:]
    fold_ref[...] = folded(both[:, :width] + mixed + mixed.T)


def grid_of(shape):
    return lax.broadcasted_iota(jnp.int32, shape, 0), lax.broadcasted_iota(jnp.int32, shape, 1)


def folded(gram):
    half = gram.shape[0] // 2
    top, bottom = gram[:half, :], gram[half:, :]
    row, column = grid_of(top.shape)
    turned = pltpu.roll(bottom, half, 1)
    main = jnp.where((column < half) & (row > column), turned, top)
    corner = jnp.sum(jnp.where(column - half == row, bottom, 0.0), axis=0, keepdims=True)
    return jnp.concatenate([main, jnp.broadcast_to(corner, (SUB, gram.shape[1]))], axis=0)


def unfolded(fold):
    half = fold.shape[1] // 2
    main = fold[:half, :]
    row, column = grid_of(main.shape)
    across = jnp.concatenate([main, jnp.zeros_like(main)], axis=0).T
    mirror = across[:half, :]
    left = column < half
    top = jnp.where(left & (row > column), mirror, main)
    turned = pltpu.roll(jnp.where(row > column, main, mirror), half, 1)
    corner = jnp.broadcast_to(fold[half : half + 1, :], main.shape)
    bottom = jnp.where(left, across[half:, :], jnp.where(column - half == row, corner, turned))
    return jnp.concatenate([top, bottom], axis=0)


def split(x):
    high = x.astype(jnp.bfloat16)
    low = (x - high.astype(jnp.float32)).astype(jnp.bfloat16)
    return high, low


def factor_inverse(gram, stage, put):
    width = gram.shape[1]
    blocks = width // SUB
    spread = lambda x: jnp.broadcast_to(x, (SUB, width))
    row, lane = grid_of((SUB, width))
    rows = [gram[i * SUB : (i + 1) * SUB, :] for i in range(blocks)]
    for b in range(blocks):
        base = b * SUB
        here = (lane >= base) & (lane < base + SUB)
        done = lane < base + SUB
        columns = [spread(rows[b][:, base + r : base + r + 1]) for r in range(SUB)]
        for j, column in enumerate(columns):
            stage[b % 2, j] = column
        m = [[spread(stage[b % 2, j, i : i + 1, :]) if j <= i else None for j in range(SUB)] for i in range(SUB)]
        own = jnp.where(here, jnp.where(lane == base + row, 1.0, 0.0), rows[b])
        p = [spread(own[r : r + 1, :]) for r in range(SUB)]
        below = range(b + 1, blocks)
        panel = {i: [spread(rows[i][:, base + r : base + r + 1]) for r in range(SUB)] for i in below}
        for i in below:
            rows[i] = jnp.where(here, 0.0, rows[i])
        for k in range(0, SUB, 2):
            a, h, c = m[k][k], m[k + 1][k], m[k + 1][k + 1]
            by_first = pl.reciprocal(a, approx=True)
            ratio = h * by_first
            det = a * c - h * h
            d = det * by_first
            by_second = a * pl.reciprocal(det, approx=True)
            p[k + 1] = p[k + 1] - ratio * p[k]
            put(base + k, jnp.where(done, p[k], 0.0), a)
            put(base + k + 1, jnp.where(done, p[k + 1], 0.0), d)
            f, t = {}, {}
            for i in range(k + 2, SUB):
                f0 = m[i][k] * by_first
                t[i] = m[i][k + 1] - f0 * h
                f[i] = (f0, t[i] * by_second)
            for j in range(k + 2, SUB):
                for i in range(j, SUB):
                    m[i][j] = (m[i][j] - f[i][0] * m[j][k]) - f[i][1] * t[j]
            for i in range(k + 2, SUB):
                p[i] = (p[i] - f[i][0] * p[k]) - f[i][1] * p[k + 1]
            for i in below:
                column = panel[i]
                f0 = column[k] * by_first
                f1 = (column[k + 1] - f0 * h) * by_second
                for j in range(k + 2, SUB):
                    column[j] = (column[j] - f0 * m[j][k]) - f1 * t[j]
                rows[i] = (rows[i] - f0 * p[k]) - f1 * p[k + 1]


def finish_kernel(total_rows, terms, halves_ref, *refs):
    term_refs, out_ref, weight, stage, made, sems = refs[:terms], *refs[terms:]
    summed = term_refs[0][...]
    for ref in term_refs[1:]:
        summed = summed + ref[...]
    width = summed.shape[1]
    row, column = grid_of((width, width))
    gram = unfolded(summed) * (1.0 / total_rows) + jnp.where(row == column, EPSILON, 0.0)

    def put(k, x, pivot):
        weight[k : k + 1, :] = (x * lax.rsqrt(pivot))[0:1, :]

    factor_inverse(gram, stage, put)
    high, low = split(weight[...].T)
    both = jnp.concatenate(
        [jnp.concatenate([high, low], axis=1), jnp.concatenate([high, jnp.zeros_like(low)], axis=1)], axis=0
    )
    copies = []
    for part in range(made.shape[0]):
        rows = slice(part * made.shape[1], (part + 1) * made.shape[1])
        product = jnp.dot(halves_ref[rows, :], both, preferred_element_type=jnp.float32)
        made[part] = product[:, :width] + product[:, width:]
        copy = pltpu.make_async_copy(made.at[part], out_ref.at[rows, :], sems.at[part])
        copy.start()
        copies.append(copy)
    for copy in copies:
        copy.wait()


def summed_over(x, axis):
    count = lax.axis_size(axis)
    if count & (count - 1):
        return [lax.psum(x, axis)]
    terms = [x]
    stride = 1
    while stride < count:
        total = functools.reduce(jnp.add, terms)
        terms = [total]
        for by in (1, 2, 3):
            if stride * by < count:
                terms.append(lax.ppermute(total, axis, [(i, i ^ (stride * by)) for i in range(count)]))
        stride *= 4
    return terms


def body(sketch, tile_values, sent_blocks, pair_counts):
    owners = lax.axis_size("shard")
    own_sketch = sketch[0]
    tiles = tile_values[0]
    rows = own_sketch.shape[0]
    plan = routes(owners)
    plan.append((list(range(owners)), [HALF] * owners, [HALF] * owners))
    block_shape = pltpu.VMEM((EXTENT, RANK), jnp.bfloat16)
    lists, counts, held, *packed = pl.pallas_call(
        functools.partial(first_pack_kernel, [plan[position][1][:4] for position in FIRST]),
        out_shape=[
            pltpu.SMEM(sent_blocks.shape, jnp.int32),
            pltpu.SMEM(pair_counts.shape, jnp.int32),
            pltpu.VMEM((rows, RANK), jnp.bfloat16),
        ]
        + [block_shape] * len(FIRST),
        in_specs=[ANY, ANY, ANY],
        out_specs=[SMEM, SMEM, VMEM] + [VMEM] * len(FIRST),
        scratch_shapes=[pltpu.SemaphoreType.DMA((3,))],
        compiler_params=pltpu.CompilerParams(vmem_limit_bytes=8 * MIB),
        name="pack_first",
    )(*[pltpu.with_memory_space_constraint(x, pltpu.HBM) for x in (sent_blocks, pair_counts, own_sketch)])
    second = [position for position in range(len(plan)) if position not in FIRST]
    lists, counts = [pltpu.with_memory_space_constraint(x, pltpu.SMEM) for x in (lists, counts)]
    if second:
        packed += pl.pallas_call(
            functools.partial(second_pack_kernel, [plan[position][1][:4] for position in second]),
            out_shape=[block_shape] * len(second),
            in_specs=[SMEM, SMEM, VMEM],
            out_specs=[VMEM] * len(second),
            compiler_params=pltpu.CompilerParams(vmem_limit_bytes=8 * MIB),
            name="pack_second",
        )(lists, counts, resident(held))
    packed = dict(zip(list(FIRST) + second, packed))
    packed = [packed[position] for position in range(len(plan))]
    arrived = []
    for (partner, _, _), block in zip(plan, packed):
        pairs = [
            (side * owners + o, (1 - side) * owners + partner[o]) for side in (0, 1) for o in range(owners)
        ]
        arrived.append(lax.ppermute(block, ("side", "shard"), pairs))
    update_shape = pltpu.VMEM((rows + TB, RANK), jnp.float32)
    halves_shape = pltpu.VMEM((rows, 2 * RANK), jnp.bfloat16)
    fold_shape = pltpu.VMEM((RANK // 2 + SUB, RANK), jnp.float32)
    tiles = resident(tiles)
    state = []
    groups = GROUPS
    for group in groups:
        last = group is groups[-1]
        kernel = last_kernel if last else next_kernel if state else first_kernel
        state = pl.pallas_call(
            functools.partial(kernel, [plan[position][2][:4] for position in group]),
            out_shape=[update_shape] + ([fold_shape, halves_shape] if last else []),
            in_specs=[SMEM, SMEM, VMEM] + [VMEM] * (len(group) + len(state)),
            out_specs=[VMEM] * (3 if last else 1),
            input_output_aliases={3 + len(group): 0} if state else {},
            compiler_params=pltpu.CompilerParams(vmem_limit_bytes=8 * MIB),
            cost_estimate=pl.CostEstimate(
                flops=2 * EXTENT * EXTENT * RANK * len(group),
                bytes_accessed=2 * EXTENT * EXTENT * len(group),
                transcendentals=0,
            ),
            name="add_pair_products",
        )(
            lists,
            counts,
            tiles,
            *[resident(arrived[position]) for position in group],
            *[resident(x) for x in state],
        )
    _, fold, halves = state
    terms = summed_over(fold, "shard")
    result = pl.pallas_call(
        functools.partial(finish_kernel, float(rows * owners), len(terms)),
        out_shape=jax.ShapeDtypeStruct((rows, RANK), jnp.float32),
        in_specs=[VMEM] * (1 + len(terms)),
        out_specs=ANY,
        scratch_shapes=[
            pltpu.VMEM((RANK, RANK), jnp.float32),
            pltpu.VMEM((2, SUB, SUB, RANK), jnp.float32),
            pltpu.VMEM((rows // CHUNK, CHUNK, RANK), jnp.float32),
            pltpu.SemaphoreType.DMA((rows // CHUNK,)),
        ],
        compiler_params=pltpu.CompilerParams(vmem_limit_bytes=8 * MIB),
        name="factor_and_apply",
    )(resident(halves), *[resident(t) for t in terms])
    return result[None]


def solution(mesh):
    return jax.shard_map(
        body,
        mesh=mesh,
        in_specs=(
            P("side", "shard", None),
            P("side", "shard", None),
            P(None, "shard"),
            P(None, "shard"),
        ),
        out_specs=P("side", "shard", None),
        check_vma=False,
    )
```

```python
import functools
import jax
import jax.numpy as jnp
from jax import lax
from jax.experimental import pallas as pl
from jax.experimental.pallas import tpu as pltpu
from jax.sharding import PartitionSpec as P

TB = 128
RANK = 128
PEER = 8
HALF = 2
PAIRS = 5
EXTENT = PEER * TB
EPSILON = 1e-05
SUB = 8
CHUNK = 256
MIB = 1 << 20
GROUPS = ((4,),(0,),(1,),(3,2))
FIRST = (0,4)

VMEM = pl.BlockSpec(memory_space=pltpu.VMEM)
SMEM = pl.BlockSpec(memory_space=pltpu.SMEM)
ANY = pl.BlockSpec(memory_space=pl.ANY)


def resident(x):
    return pltpu.with_memory_space_constraint(x, pltpu.VMEM)


def routes(owners):
    if owners % 4 == 0:
        up = [
            lambda o: (o // 2) % 2 == 0,
            lambda o: o % 2 == 1,
            lambda o: (o // 2) % 2 == 1,
            lambda o: o % 2 == 0,
        ]
        reach = [2, 1, 2, 1]
        made = []
        for is_up, by in zip(up, reach):
            partner = [(o + (by if is_up(o) else -by)) % owners for o in range(owners)]
            pair = [HALF + (by if is_up(o) else -by) for o in range(owners)]
            made.append((partner, pair, pair))
        return made
    made = []
    for by in (2, 1, -2, -1):
        partner = [(o + by) % owners for o in range(owners)]
        made.append((partner, [HALF + by] * owners, [HALF - by] * owners))
    return made


def pair_position(table, owner):
    value = table[3]
    for place in (2, 1, 0):
        value = jnp.where(lax.rem(owner, 4) == place, table[place], value)
    return value


def pack(tables, lists, counts, sketch, out_refs):
    side = lax.axis_index("side")
    owner = lax.axis_index("shard")
    for table, out_ref in zip(tables, out_refs):
        pair = pair_position(table, owner)
        live = counts[side, pair]
        for slot in range(PEER):
            start = pl.multiple_of(lists[side, pair * PEER + slot] * TB, TB)
            block = sketch[pl.ds(start, TB), :]
            out_ref[slot * TB : (slot + 1) * TB, :] = jnp.where(slot < live, block, jnp.zeros_like(block))


def first_pack_kernel(tables, lists_ref, counts_ref, sketch_ref, lists, counts, held, *refs):
    out_refs, sems = refs[:-1], refs[-1]
    copies = [
        pltpu.make_async_copy(source, target, sems.at[i])
        for i, (source, target) in enumerate(((sketch_ref, held), (lists_ref, lists), (counts_ref, counts)))
    ]
    for copy in copies:
        copy.start()
    for copy in copies[::-1]:
        copy.wait()
    pack(tables, lists, counts, held, out_refs)


def second_pack_kernel(tables, lists, counts, held, *out_refs):
    pack(tables, lists, counts, held, out_refs)


def add_product(table, lists_ref, counts_ref, tile_ref, fetched_ref, update_ref):
    side = lax.axis_index("side")
    pair = pair_position(table, lax.axis_index("shard"))
    live = counts_ref[side, pair]
    unused = update_ref.shape[0] // TB - 1
    fetched = fetched_ref[...]
    for first in range(0, PEER, CHUNK // TB):
        start = pl.multiple_of(pair * EXTENT + first * TB, CHUNK)
        part = jnp.dot(tile_ref[pl.ds(start, CHUNK), :], fetched, preferred_element_type=jnp.float32)
        for step in range(CHUNK // TB):
            slot = first + step
            block = jnp.where(slot < live, lists_ref[side, pair * PEER + slot], unused)
            rows = pl.ds(pl.multiple_of(block * TB, TB), TB)
            update_ref[rows, :] += part[step * TB : (step + 1) * TB, :]


def first_kernel(tables, lists_ref, counts_ref, tile_ref, *refs):
    fetched_refs, update_ref = refs[: len(tables)], refs[len(tables)]
    update_ref[...] = jnp.zeros_like(update_ref)
    for table, fetched_ref in zip(tables, fetched_refs):
        add_product(table, lists_ref, counts_ref, tile_ref, fetched_ref, update_ref)


def next_kernel(tables, lists_ref, counts_ref, tile_ref, *refs):
    fetched_refs, (_, update_ref) = refs[: len(tables)], refs[len(tables) :]
    for table, fetched_ref in zip(tables, fetched_refs):
        add_product(table, lists_ref, counts_ref, tile_ref, fetched_ref, update_ref)


def last_kernel(tables, lists_ref, counts_ref, tile_ref, *refs):
    fetched_refs, (_, update_ref, fold_ref, halves_ref) = refs[: len(tables)], refs[len(tables) :]
    for table, fetched_ref in zip(tables, fetched_refs):
        add_product(table, lists_ref, counts_ref, tile_ref, fetched_ref, update_ref)
    rows, width = halves_ref.shape[0], halves_ref.shape[1] // 2
    high, low = split(update_ref[:rows, :])
    halves_ref[:, :width] = high
    halves_ref[:, width:] = low
    both = lax.dot_general(
        high, halves_ref[...], (((0,), (0,)), ((), ())), preferred_element_type=jnp.float32
    )
    mixed = both[:, width:]
    fold_ref[...] = folded(both[:, :width] + mixed + mixed.T)


def grid_of(shape):
    return lax.broadcasted_iota(jnp.int32, shape, 0), lax.broadcasted_iota(jnp.int32, shape, 1)


def folded(gram):
    half = gram.shape[0] // 2
    top, bottom = gram[:half, :], gram[half:, :]
    row, column = grid_of(top.shape)
    turned = pltpu.roll(bottom, half, 1)
    main = jnp.where((column < half) & (row > column), turned, top)
    corner = jnp.sum(jnp.where(column - half == row, bottom, 0.0), axis=0, keepdims=True)
    return jnp.concatenate([main, jnp.broadcast_to(corner, (SUB, gram.shape[1]))], axis=0)


def unfolded(fold):
    half = fold.shape[1] // 2
    main = fold[:half, :]
    row, column = grid_of(main.shape)
    across = jnp.concatenate([main, jnp.zeros_like(main)], axis=0).T
    mirror = across[:half, :]
    left = column < half
    top = jnp.where(left & (row > column), mirror, main)
    turned = pltpu.roll(jnp.where(row > column, main, mirror), half, 1)
    corner = jnp.broadcast_to(fold[half : half + 1, :], main.shape)
    bottom = jnp.where(left, across[half:, :], jnp.where(column - half == row, corner, turned))
    return jnp.concatenate([top, bottom], axis=0)


def split(x):
    high = x.astype(jnp.bfloat16)
    low = (x - high.astype(jnp.float32)).astype(jnp.bfloat16)
    return high, low


def factor_inverse(gram, stage, put):
    width = gram.shape[1]
    blocks = width // SUB
    spread = lambda x: jnp.broadcast_to(x, (SUB, width))
    row, lane = grid_of((SUB, width))
    rows = [gram[i * SUB : (i + 1) * SUB, :] for i in range(blocks)]
    for b in range(blocks):
        base = b * SUB
        here = (lane >= base) & (lane < base + SUB)
        done = lane < base + SUB
        columns = [spread(rows[b][:, base + r : base + r + 1]) for r in range(SUB)]
        for j, column in enumerate(columns):
            stage[b % 2, j] = column
        m = [[spread(stage[b % 2, j, i : i + 1, :]) if j <= i else None for j in range(SUB)] for i in range(SUB)]
        own = jnp.where(here, jnp.where(lane == base + row, 1.0, 0.0), rows[b])
        p = [spread(own[r : r + 1, :]) for r in range(SUB)]
        below = range(b + 1, blocks)
        panel = {i: [spread(rows[i][:, base + r : base + r + 1]) for r in range(SUB)] for i in below}
        for i in below:
            rows[i] = jnp.where(here, 0.0, rows[i])
        for k in range(0, SUB, 2):
            a, h, c = m[k][k], m[k + 1][k], m[k + 1][k + 1]
            by_first = pl.reciprocal(a, approx=True)
            ratio = h * by_first
            det = a * c - h * h
            d = det * by_first
            by_det = pl.reciprocal(det, approx=True)
            p[k + 1] = p[k + 1] - ratio * p[k]
            put(base + k, jnp.where(done, p[k], 0.0), a)
            put(base + k + 1, jnp.where(done, p[k + 1], 0.0), d)
            f, t = {}, {}
            for i in range(k + 2, SUB):
                f0 = m[i][k] * by_first
                t[i] = m[i][k + 1] - f0 * h
                f[i] = (f0, (a * m[i][k + 1] - h * m[i][k]) * by_det)
            for j in range(k + 2, SUB):
                for i in range(j, SUB):
                    m[i][j] = (m[i][j] - f[i][0] * m[j][k]) - f[i][1] * t[j]
            for i in range(k + 2, SUB):
                p[i] = (p[i] - f[i][0] * p[k]) - f[i][1] * p[k + 1]
            for i in below:
                column = panel[i]
                f0 = column[k] * by_first
                f1 = (a * column[k + 1] - h * column[k]) * by_det
                for j in range(k + 2, SUB):
                    column[j] = (column[j] - f0 * m[j][k]) - f1 * t[j]
                rows[i] = (rows[i] - f0 * p[k]) - f1 * p[k + 1]


def finish_kernel(total_rows, terms, halves_ref, *refs):
    term_refs, out_ref, weight, stage, made, sems = refs[:terms], *refs[terms:]
    summed = term_refs[0][...]
    for ref in term_refs[1:]:
        summed = summed + ref[...]
    width = summed.shape[1]
    row, column = grid_of((width, width))
    gram = unfolded(summed) * (1.0 / total_rows) + jnp.where(row == column, EPSILON, 0.0)

    def put(k, x, pivot):
        weight[k : k + 1, :] = (x * lax.rsqrt(pivot))[0:1, :]

    factor_inverse(gram, stage, put)
    high, low = split(weight[...].T)
    both = jnp.concatenate(
        [jnp.concatenate([high, low], axis=1), jnp.concatenate([high, jnp.zeros_like(low)], axis=1)], axis=0
    )
    copies = []
    for part in range(made.shape[0]):
        rows = slice(part * made.shape[1], (part + 1) * made.shape[1])
        product = jnp.dot(halves_ref[rows, :], both, preferred_element_type=jnp.float32)
        made[part] = product[:, :width] + product[:, width:]
        copy = pltpu.make_async_copy(made.at[part], out_ref.at[rows, :], sems.at[part])
        copy.start()
        copies.append(copy)
    for copy in copies:
        copy.wait()


def summed_over(x, axis):
    count = lax.axis_size(axis)
    if count & (count - 1):
        return [lax.psum(x, axis)]
    terms = [x]
    stride = 1
    while stride < count:
        total = functools.reduce(jnp.add, terms)
        terms = [total]
        for by in (1, 2, 3):
            if stride * by < count:
                terms.append(lax.ppermute(total, axis, [(i, i ^ (stride * by)) for i in range(count)]))
        stride *= 4
    return terms


def body(sketch, tile_values, sent_blocks, pair_counts):
    owners = lax.axis_size("shard")
    own_sketch = sketch[0]
    tiles = tile_values[0]
    rows = own_sketch.shape[0]
    plan = routes(owners)
    plan.append((list(range(owners)), [HALF] * owners, [HALF] * owners))
    block_shape = pltpu.VMEM((EXTENT, RANK), jnp.bfloat16)
    lists, counts, held, *packed = pl.pallas_call(
        functools.partial(first_pack_kernel, [plan[position][1][:4] for position in FIRST]),
        out_shape=[
            pltpu.SMEM(sent_blocks.shape, jnp.int32),
            pltpu.SMEM(pair_counts.shape, jnp.int32),
            pltpu.VMEM((rows, RANK), jnp.bfloat16),
        ]
        + [block_shape] * len(FIRST),
        in_specs=[ANY, ANY, ANY],
        out_specs=[SMEM, SMEM, VMEM] + [VMEM] * len(FIRST),
        scratch_shapes=[pltpu.SemaphoreType.DMA((3,))],
        compiler_params=pltpu.CompilerParams(vmem_limit_bytes=8 * MIB),
        name="pack_first",
    )(*[pltpu.with_memory_space_constraint(x, pltpu.HBM) for x in (sent_blocks, pair_counts, own_sketch)])
    second = [position for position in range(len(plan)) if position not in FIRST]
    lists, counts = [pltpu.with_memory_space_constraint(x, pltpu.SMEM) for x in (lists, counts)]
    if second:
        packed += pl.pallas_call(
            functools.partial(second_pack_kernel, [plan[position][1][:4] for position in second]),
            out_shape=[block_shape] * len(second),
            in_specs=[SMEM, SMEM, VMEM],
            out_specs=[VMEM] * len(second),
            compiler_params=pltpu.CompilerParams(vmem_limit_bytes=8 * MIB),
            name="pack_second",
        )(lists, counts, resident(held))
    packed = dict(zip(list(FIRST) + second, packed))
    packed = [packed[position] for position in range(len(plan))]
    arrived = []
    for (partner, _, _), block in zip(plan, packed):
        pairs = [
            (side * owners + o, (1 - side) * owners + partner[o]) for side in (0, 1) for o in range(owners)
        ]
        arrived.append(lax.ppermute(block, ("side", "shard"), pairs))
    update_shape = pltpu.VMEM((rows + TB, RANK), jnp.float32)
    halves_shape = pltpu.VMEM((rows, 2 * RANK), jnp.bfloat16)
    fold_shape = pltpu.VMEM((RANK // 2 + SUB, RANK), jnp.float32)
    tiles = resident(tiles)
    state = []
    groups = GROUPS
    for group in groups:
        last = group is groups[-1]
        kernel = last_kernel if last else next_kernel if state else first_kernel
        state = pl.pallas_call(
            functools.partial(kernel, [plan[position][2][:4] for position in group]),
            out_shape=[update_shape] + ([fold_shape, halves_shape] if last else []),
            in_specs=[SMEM, SMEM, VMEM] + [VMEM] * (len(group) + len(state)),
            out_specs=[VMEM] * (3 if last else 1),
            input_output_aliases={3 + len(group): 0} if state else {},
            compiler_params=pltpu.CompilerParams(vmem_limit_bytes=8 * MIB),
            cost_estimate=pl.CostEstimate(
                flops=2 * EXTENT * EXTENT * RANK * len(group),
                bytes_accessed=2 * EXTENT * EXTENT * len(group),
                transcendentals=0,
            ),
            name="add_pair_products",
        )(
            lists,
            counts,
            tiles,
            *[resident(arrived[position]) for position in group],
            *[resident(x) for x in state],
        )
    _, fold, halves = state
    terms = summed_over(fold, "shard")
    result = pl.pallas_call(
        functools.partial(finish_kernel, float(rows * owners), len(terms)),
        out_shape=jax.ShapeDtypeStruct((rows, RANK), jnp.float32),
        in_specs=[VMEM] * (1 + len(terms)),
        out_specs=ANY,
        scratch_shapes=[
            pltpu.VMEM((RANK, RANK), jnp.float32),
            pltpu.VMEM((2, SUB, SUB, RANK), jnp.float32),
            pltpu.VMEM((rows // CHUNK, CHUNK, RANK), jnp.float32),
            pltpu.SemaphoreType.DMA((rows // CHUNK,)),
        ],
        compiler_params=pltpu.CompilerParams(vmem_limit_bytes=8 * MIB),
        name="factor_and_apply",
    )(resident(halves), *[resident(t) for t in terms])
    return result[None]


def solution(mesh):
    return jax.shard_map(
        body,
        mesh=mesh,
        in_specs=(
            P("side", "shard", None),
            P("side", "shard", None),
            P(None, "shard"),
            P(None, "shard"),
        ),
        out_specs=P("side", "shard", None),
        check_vma=False,
    )
```
